768 devices in a mesh: dp: 12 (over z), node: 8 (over x, core), local: 8 (over y).
Axes of the slice: x: 4, y: 8, z: 12, core: 2. Of those that a mesh axis runs over, the one named last changes fastest.
Arguments:
- tokens: bfloat16 [98304, 2048], P(('dp', 'node', 'local')), may hold values from -6 to 6
- expert_ids: int32 [98304, 1], P(('dp', 'node', 'local')), may hold values from 0 to 63; in each aligned block of 128 rows (0 to 127, 128 to 255, ...) at most 4 rows name the same one
- gates: float32 [98304, 1], P(('dp', 'node', 'local')), may hold values from 0.05 to 1
- out_grad: bfloat16 [98304, 2048], P(('dp', 'node', 'local')), may hold values from -1.1953125 to 1.1953125
- w_gate: bfloat16 [64, 2048, 384], P(('node', 'local')), may hold values from -0.125 to 0.125
- w_up: bfloat16 [64, 2048, 384], P(('node', 'local')), may hold values from -0.125 to 0.125
- w_down: bfloat16 [64, 384, 2048], P(('node', 'local')), may hold values from -0.3125 to 0.3125
Outputs:
- layer_out: bfloat16 [98304, 2048], P(('dp', 'node', 'local'))
- grad_in: bfloat16 [98304, 2048], P(('dp', 'node', 'local'))
- grad_gates: float32 [98304, 1], P(('dp', 'node', 'local'))
- grad_w_gate: bfloat16 [64, 384, 2048], P(('node', 'local'), 'dp')
- grad_w_up: bfloat16 [64, 384, 2048], P(('node', 'local'), 'dp')
- grad_w_down: bfloat16 [64, 384, 2048], P(('node', 'local'), 'dp')
The draws below stay inside these ranges and needn't reach their ends.
Inputs may be any that keep to these rules, and one draw needn't show every extreme that they name: `expert_ids`: each token names one expert; among the tokens of one device no expert is named more than 4 times, and in some device one expert is named exactly 4 times; every expert is named somewhere.
All inputs are finite; a program needn't handle non-finite values.
Results may differ from the reference program's by a relative error of at most 0.02.
Values may be sent and summed in bfloat16 or wider, within the bound.
No kernel may reach another device: no remote copies, remote signals or barrier semaphores. Data moves between devices by JAX's collectives and lax.ppermute only.
A program may use at most 64 MiB of HBM per device.

```python
import math
import jax
import jax.numpy as jnp
import numpy as np
from jax import lax

D = 2048
FH = 384
TOPK = 1
TOK_DEV = 128
EXPERTS = 64
CAP = 4
TOKENS = 98304
N_DP = 12
DEVICES = 768


def shard_levels(stream_key, dims, cuts, low, largest):
    def one(dim, blocks):
        heights = jax.random.uniform(jax.random.fold_in(jax.random.fold_in(stream_key, 6), dim), (blocks,), jnp.float32, low / len(cuts), largest / len(cuts))
        return jnp.repeat(jnp.exp(heights), dims[dim] // blocks).reshape((-1,) + (1,) * (len(dims) - dim - 1))

    factor_of = one(*cuts[0])
    for cut in cuts[1:]:
        factor_of = factor_of * one(*cut)
    return factor_of


def assign_block(stream_key, own, number, rows, amount, top, bound, lean):
    order = jax.random.permutation(stream_key, amount)
    packed, usual = portions_of(amount, rows * top, bound, lean, True), portions_of(amount, rows * top, bound, lean, False)
    places = jnp.arange(amount)

    def named(lengths, offset_by):
        used = int((lengths > 0).sum())
        fixed = max(1, used // 4)
        shifted = fixed + (places - fixed + offset_by * (used - fixed)) % max(1, amount - fixed)
        return jnp.zeros((amount,), jnp.int32).at[order[jnp.where(places < fixed, places, shifted)]].set(jnp.asarray(lengths, jnp.int32))

    lengths = jnp.where(number % 4 == 0, named(packed, number // 4), named(usual, number - number // 4 - 1))
    mixed = jax.random.permutation(jax.random.fold_in(own, 3), amount)
    source_of, sink = mixed[0:amount // 2 * 2:2], mixed[1:amount // 2 * 2:2]
    margin = jnp.minimum(lengths[source_of] - 1, bound - lengths[sink]) // 2
    margin = jnp.where((source_of == order[0]) | (sink == order[0]) | (lengths[sink] == 0), 0, jnp.maximum(margin, 0))
    shifted = jax.random.randint(jax.random.fold_in(own, 4), (amount // 2,), 0, 1 << 20) % (margin + 1)
    lengths = lengths.at[source_of].add(-shifted).at[sink].add(shifted)
    members = jnp.searchsorted(jnp.cumsum(lengths), jnp.arange(rows * top), side="right").astype(jnp.int32)
    grid = members.reshape(top, rows).T
    grid = grid[jax.random.permutation(jax.random.fold_in(own, 1), rows)]
    offset_by = jax.random.randint(jax.random.fold_in(own, 2), (rows, 1), 0, top)
    return jnp.take_along_axis(grid, (jnp.arange(top)[None, :] + offset_by) % top, axis=1)


def portions_of(number_of, total, most, lean, full):
    portions = [(1 << 20) // math.isqrt(standing ** lean) + 1 for standing in range(1, number_of + 1)]
    largest = most if full else min(most, max(-(-total // number_of), total * portions[0] // sum(portions)))
    least = 1 if total - largest >= number_of - 1 else 0
    holding, surplus = [largest] + [least] * (number_of - 1), total - largest - least * (number_of - 1)
    while surplus > 0:
        candidates = [i for i in range(1, number_of) if holding[i] < largest] or [i for i in range(1, number_of) if holding[i] < most]
        whole, budget = sum([portions[i] for i in candidates]), surplus
        for i in candidates:
            addition = min(most - holding[i], max(1, budget * portions[i] // whole), surplus)
            holding[i] = holding[i] + addition
            surplus = surplus - addition
    return np.array(holding)


def gaussian(own_key, shape, scale, limit, split=(), kind=jnp.bfloat16):
    gain = shard_levels(own_key, shape, split, -0.22, 0.18) if split else 1.0
    values = jax.random.normal(own_key, shape, jnp.float32) * scale * gain
    return jnp.minimum(jnp.maximum(values, -limit), limit).astype(kind)


def setup_inputs(seed: int = 0) -> dict:
    splits = jax.random.split(jax.random.key(seed), 8)
    tokens = gaussian(splits[0], (TOKENS, D), 1.0, 6.0, ((0, 768),))
    expert_ids_keys = jax.random.split(jax.random.fold_in(splits[1], 1), TOKENS // TOK_DEV)
    expert_ids_turns = jax.random.permutation(jax.random.fold_in(splits[1], 3), TOKENS // TOK_DEV)
    expert_ids = jax.vmap(lambda own, number: assign_block(jax.random.fold_in(splits[1], 2), own, number, TOK_DEV, EXPERTS, TOPK, CAP, 2))(expert_ids_keys, expert_ids_turns).reshape((TOKENS, TOPK))
    gates = jnp.clip(jnp.exp(math.log(1.0) - 2.9957323 * jax.random.uniform(splits[2], (TOKENS, TOPK), jnp.float32) ** shard_levels(splits[2], (TOKENS, TOPK), ((0, 768),), -0.2, 0.2)), 0.05, 1.0)
    out_grad = gaussian(splits[3], (TOKENS, D), 0.2, 1.1953125, ((0, 768),))
    w_gate = gaussian(splits[4], (EXPERTS, D, FH), D ** -0.5, 0.125, ((0, 64),))
    w_up = gaussian(splits[5], (EXPERTS, D, FH), D ** -0.5, 0.125, ((0, 64),))
    w_down = gaussian(splits[6], (EXPERTS, FH, D), FH ** -0.5, 0.3125, ((0, 64),))
    return dict(tokens=tokens, expert_ids=expert_ids, gates=gates, out_grad=out_grad, w_gate=w_gate, w_up=w_up, w_down=w_down)


def silu_parts(pre_gate):
    sigma = jax.nn.sigmoid(pre_gate)
    return pre_gate * sigma, sigma * (1.0 + pre_gate * (1.0 - sigma))


def per_replica(factor, operand):
    first = factor.astype(jnp.float32).reshape(N_DP, EXPERTS * CAP, factor.shape[1])
    second = operand.astype(jnp.float32).reshape(N_DP, EXPERTS * CAP, operand.shape[1])
    terms = jnp.einsum("rnf,rnd->rfd", first, second)
    rounded = lax.optimization_barrier(terms.astype(jnp.bfloat16))
    return jnp.sum(rounded.astype(jnp.float32), axis=0).astype(jnp.bfloat16)


def reference(tokens, expert_ids, gates, out_grad, w_gate, w_up, w_down):
    total_rows = TOKENS * TOPK
    flat_ids = expert_ids.reshape(DEVICES, TOK_DEV * TOPK)
    onehot = (flat_ids[:, :, None] == jnp.arange(EXPERTS, dtype=jnp.int32)[None, None, :]).astype(jnp.int32)
    rank = jnp.cumsum(onehot, axis=1) - onehot
    slot = jnp.sum(rank * onehot, axis=2).astype(jnp.int32)
    device = jnp.arange(DEVICES, dtype=jnp.int32)[:, None]
    position = device * CAP + slot
    assign = jnp.arange(total_rows, dtype=jnp.int32).reshape(DEVICES, TOK_DEV * TOPK)
    anchor = jnp.full((EXPERTS, DEVICES * CAP), total_rows, jnp.int32).at[flat_ids, position].set(assign)
    flat_gates = gates.reshape(total_rows)

    def expert_step(carry, items):
        out_acc, grad_acc, gate_acc = carry
        rows_of, weight_gate, weight_up, weight_down = items
        live = rows_of < total_rows
        clipped = jnp.minimum(rows_of, total_rows - 1)
        token_of = clipped // TOPK
        gate_of = jnp.where(live, flat_gates[clipped], jnp.zeros((), flat_gates.dtype))
        expert_in = jnp.where(live[:, None], tokens[token_of], jnp.zeros((), tokens.dtype))
        pre_gate = jnp.dot(expert_in, weight_gate, preferred_element_type=jnp.float32)
        pre_up = jnp.dot(expert_in, weight_up, preferred_element_type=jnp.float32)
        activated, slope = silu_parts(pre_gate)
        hidden = (activated * pre_up).astype(jnp.bfloat16)
        expert_out = jnp.dot(hidden, weight_down, preferred_element_type=jnp.float32).astype(jnp.bfloat16)
        grad_rows = out_grad[token_of].astype(jnp.float32)
        out_acc = out_acc.at[token_of].add(gate_of[:, None] * expert_out.astype(jnp.float32))
        gate_value = jnp.sum(grad_rows * expert_out.astype(jnp.float32), axis=1)
        gate_acc = gate_acc.at[clipped].add(jnp.where(live, gate_value, jnp.zeros((), gate_value.dtype)))
        expert_grad = (gate_of[:, None] * grad_rows).astype(jnp.bfloat16)
        grad_hidden = jnp.dot(expert_grad, weight_down.T, preferred_element_type=jnp.float32)
        grad_pre_gate = (grad_hidden * pre_up * slope).astype(jnp.bfloat16)
        grad_pre_up = (grad_hidden * activated).astype(jnp.bfloat16)
        input_grad = (jnp.dot(grad_pre_gate, weight_gate.T, preferred_element_type=jnp.float32)
                      + jnp.dot(grad_pre_up, weight_up.T, preferred_element_type=jnp.float32)).astype(jnp.bfloat16)
        grad_acc = grad_acc.at[token_of].add(input_grad.astype(jnp.float32))
        sums = (per_replica(grad_pre_gate, expert_in), per_replica(grad_pre_up, expert_in), per_replica(hidden, expert_grad))
        return (out_acc, grad_acc, gate_acc), sums

    start = (jnp.zeros((TOKENS, D), jnp.float32), jnp.zeros((TOKENS, D), jnp.float32), jnp.zeros((total_rows,), jnp.float32))
    final, stacked = lax.scan(expert_step, start, (anchor, w_gate, w_up, w_down))
    out_acc, grad_acc, gate_acc = final
    return (out_acc.astype(jnp.bfloat16), grad_acc.astype(jnp.bfloat16), gate_acc.reshape(TOKENS, TOPK),
            stacked[0], stacked[1], stacked[2])
```

```python
import functools

import jax
import jax.numpy as jnp
from jax import lax
from jax.experimental import pallas as pl
from jax.experimental.pallas import tpu as pltpu
from jax.sharding import PartitionSpec as P

BF16 = jnp.bfloat16
F32 = jnp.float32
VMEM = pl.BlockSpec(memory_space=pltpu.VMEM)


def dot(a, b, da, db):
    return lax.dot_general(a, b, (((da,), (db,)), ((), ())), preferred_element_type=F32)


def iota(shape, dim):
    return lax.broadcasted_iota(jnp.int32, shape, dim)


def slots_of(ids, experts, capacity):
    tok = ids.shape[1]
    named = iota((experts, tok), 0) == ids
    before = (iota((tok, tok), 0) < iota((tok, tok), 1)).astype(BF16)
    rank = dot(named.astype(BF16), before, 1, 0)
    place = jnp.sum(jnp.where(named, rank, 0.0), axis=0, keepdims=True).astype(jnp.int32)
    return ids * (2 * capacity) + place


def column_of(row):
    tok = row.shape[1]
    eye = iota((tok, tok), 0) == iota((tok, tok), 1)
    return jnp.sum(jnp.where(eye, row, 0.0), axis=1, keepdims=True)


def hot(target, rows):
    return (iota((rows, target.shape[1]), 0) == target).astype(F32).astype(BF16)


def dispatch_kernel(experts, capacity, ids_ref, gates_ref, tokens_ref, grad_ref, out_ref):
    target = slots_of(ids_ref[...], experts, capacity)
    gates = column_of(gates_ref[...])
    scaled = (gates * grad_ref[...].astype(F32)).astype(BF16)
    rows = 2 * capacity * experts
    out = dot(hot(target, rows), tokens_ref[...], 1, 0)
    out += dot(hot(target + capacity, rows), scaled, 1, 0)
    out_ref[...] = out.astype(BF16)


def pick(rows, capacity, kind):
    at, of = iota((rows, 2 * rows), 0), iota((rows, 2 * rows), 1)
    return (of == at + (at // capacity + kind) * capacity).astype(F32).astype(BF16)


def terms_kernel(
    capacity, parts, in_ref, gate_ref, up_ref, down_ref, terms_ref, hidden_ref, dgate_ref, dup_ref
):
    rows = in_ref.shape[0] // 2
    both = in_ref[...]
    incoming = dot(pick(rows, capacity, 0), both, 1, 0).astype(BF16)
    expert_grad = dot(pick(rows, capacity, 1), both, 1, 0).astype(BF16)
    pre_gate = dot(incoming, gate_ref[0], 1, 0)
    pre_up = dot(incoming, up_ref[0], 1, 0)
    sigma = jax.nn.sigmoid(pre_gate)
    activated = pre_gate * sigma
    slope = sigma * (1.0 + pre_gate * (1.0 - sigma))
    hidden = (activated * pre_up).astype(BF16)
    grad_hidden = dot(expert_grad, down_ref[0], 1, 1)
    dgate = (grad_hidden * pre_up * slope).astype(BF16)
    dup = (grad_hidden * activated).astype(BF16)
    hidden_ref[...] = hidden
    dgate_ref[...] = dgate
    dup_ref[...] = dup
    for k, (factor, operand) in enumerate(
        ((dgate, incoming), (dup, incoming), (hidden, expert_grad))
    ):
        term = dot(factor, operand, 0, 0).astype(BF16)
        terms_ref[:, k] = term.reshape(parts, term.shape[0] // parts, term.shape[1])


def returns_kernel(capacity, hidden_ref, dgate_ref, dup_ref, gate_ref, up_ref, down_ref, out_ref):
    rows = hidden_ref.shape[0]
    back = dot(hidden_ref[...], down_ref[0], 1, 0).astype(BF16)
    grad = (
        dot(dgate_ref[...], gate_ref[0], 1, 1) + dot(dup_ref[...], up_ref[0], 1, 1)
    ).astype(BF16)
    out = dot(pick(rows, capacity, 0), back, 0, 0) + dot(pick(rows, capacity, 1), grad, 0, 0)
    out_ref[...] = out.astype(BF16)


def combine_kernel(
    experts, capacity, ids_ref, gates_ref, grad_ref, back_ref, out_ref, dtok_ref, dgates_ref
):
    target = slots_of(ids_ref[...], experts, capacity)
    gates = column_of(gates_ref[...])
    rows = 2 * capacity * experts
    back = back_ref[...]
    slot_out = dot(hot(target, rows), back, 0, 0)
    dtok_ref[...] = dot(hot(target + capacity, rows), back, 0, 0).astype(BF16)
    out_ref[...] = (gates * slot_out).astype(BF16)
    value = jnp.sum(grad_ref[...].astype(F32) * slot_out, axis=1, keepdims=True)
    tok = value.shape[0]
    eye = iota((tok, tok), 0) == iota((tok, tok), 1)
    dgates_ref[...] = jnp.sum(jnp.where(eye, value, 0.0), axis=0, keepdims=True)


def call(kernel, out_shape, n_in, flops, traffic, name):
    many = isinstance(out_shape, (tuple, list))
    return pl.pallas_call(
        kernel,
        out_shape=out_shape,
        in_specs=[VMEM] * n_in,
        out_specs=[VMEM] * len(out_shape) if many else VMEM,
        compiler_params=pltpu.CompilerParams(vmem_limit_bytes=32 * 2**20),
        cost_estimate=pl.CostEstimate(flops=flops, bytes_accessed=traffic, transcendentals=0),
        name=name,
    )


def move_rows(buffer):
    return lax.all_to_all(buffer, ("node", "local"), split_axis=0, concat_axis=0, tiled=True)


def on_device(tokens, expert_ids, gates, out_grad, w_gate, w_up, w_down):
    experts = lax.axis_size("node") * lax.axis_size("local")
    parts = lax.axis_size("dp")
    tok, width = tokens.shape
    units = w_gate.shape[2]
    capacity = max(2, 2 * tok // experts)
    rows = experts * capacity
    sds = jax.ShapeDtypeStruct
    ids = expert_ids.reshape(1, tok)
    gate_row = gates.reshape(1, tok)
    outgoing = call(
        functools.partial(dispatch_kernel, experts, capacity),
        sds((2 * rows, width), BF16), 4, 8 * rows * tok * width, 8 * tok * width, "dispatch",
    )(ids, gate_row, tokens, out_grad)
    incoming = move_rows(outgoing.reshape(experts, 2 * capacity, width)).reshape(2 * rows, width)
    small = sds((rows, units), BF16)
    terms, hidden, dgate, dup = call(
        functools.partial(terms_kernel, capacity, parts),
        (sds((parts, 3, units // parts, width), BF16), small, small, small),
        4, 18 * rows * width * units, 10 * width * units + 4 * rows * width, "terms",
    )(incoming, w_gate, w_up, w_down)
    shares = lax.psum_scatter(
        terms.reshape(3 * units, width), "dp", scatter_dimension=0, tiled=True
    )
    back = call(
        functools.partial(returns_kernel, capacity),
        sds((2 * rows, width), BF16), 6, 10 * rows * width * units,
        6 * width * units + 4 * rows * width, "returns",
    )(hidden, dgate, dup, w_gate, w_up, w_down)
    back = move_rows(back.reshape(experts, 2 * capacity, width)).reshape(2 * rows, width)
    layer_out, grad_in, grad_gates = call(
        functools.partial(combine_kernel, experts, capacity),
        (sds((tok, width), BF16), sds((tok, width), BF16), sds((1, tok), F32)),
        4, 8 * rows * tok * width, 10 * tok * width, "combine",
    )(ids, gate_row, out_grad, back)
    part = units // parts
    return (
        layer_out,
        grad_in,
        grad_gates.reshape(tok, 1),
        shares[None, :part],
        shares[None, part : 2 * part],
        shares[None, 2 * part :],
    )


def solution(mesh):
    by_token = P(("dp", "node", "local"), None)
    by_expert = P(("node", "local"), None, None)
    by_share = P(("node", "local"), "dp", None)
    return jax.shard_map(
        on_device,
        mesh=mesh,
        in_specs=(by_token,) * 4 + (by_expert,) * 3,
        out_specs=(by_token,) * 3 + (by_share,) * 3,
        check_vma=False,
    )
```

```python
import functools

import jax
import jax.numpy as jnp
from jax import lax
from jax.experimental import pallas as pl
from jax.experimental.pallas import tpu as pltpu
from jax.sharding import PartitionSpec as P

BF16 = jnp.bfloat16
F32 = jnp.float32
VMEM = pl.BlockSpec(memory_space=pltpu.VMEM)
HBM = pl.BlockSpec(memory_space=pltpu.HBM)


def dot(a, b, da, db):
    return lax.dot_general(a, b, (((da,), (db,)), ((), ())), preferred_element_type=F32)


def iota(shape, dim):
    return lax.broadcasted_iota(jnp.int32, shape, dim)


def slots_of(ids, experts, capacity):
    tok = ids.shape[1]
    named = iota((experts, tok), 0) == ids
    before = (iota((tok, tok), 0) < iota((tok, tok), 1)).astype(BF16)
    rank = dot(named.astype(BF16), before, 1, 0)
    place = jnp.sum(jnp.where(named, rank, 0.0), axis=0, keepdims=True).astype(jnp.int32)
    return ids * (2 * capacity) + place


def column_of(row):
    tok = row.shape[1]
    eye = iota((tok, tok), 0) == iota((tok, tok), 1)
    return jnp.sum(jnp.where(eye, row, 0.0), axis=1, keepdims=True)


def hot(target, rows):
    return (iota((rows, target.shape[1]), 0) == target).astype(F32).astype(BF16)


def dispatch_kernel(
    experts, capacity, ids_hbm, gates_hbm, tokens_hbm, grad_hbm, out_ref,
    ids_ref, gates_ref, tokens_ref, grad_ref, sems,
):
    loads = [
        pltpu.make_async_copy(src, dst, sems.at[i])
        for i, (src, dst) in enumerate((
            (ids_hbm, ids_ref), (gates_hbm, gates_ref), (tokens_hbm, tokens_ref), (grad_hbm, grad_ref)
        ))
    ]
    for load in loads:
        load.start()
    loads[0].wait()
    target = slots_of(ids_ref[...], experts, capacity)
    rows = 2 * capacity * experts
    to_token, to_grad = hot(target, rows), hot(target + capacity, rows)
    loads[1].wait()
    gates = column_of(gates_ref[...])
    loads[2].wait()
    out = dot(to_token, tokens_ref[...], 1, 0)
    loads[3].wait()
    scaled = (gates * grad_ref[...].astype(F32)).astype(BF16)
    out += dot(to_grad, scaled, 1, 0)
    out_ref[...] = out.astype(BF16)


def pick(rows, capacity, kind):
    at, of = iota((rows, 2 * rows), 0), iota((rows, 2 * rows), 1)
    return (of == at + (at // capacity + kind) * capacity).astype(F32).astype(BF16)


def terms_kernel(
    capacity, parts, in_ref, gate_ref, up_ref, down_ref, terms_hbm, factors_hbm,
    terms_ref, factors_ref, sems,
):
    rows = in_ref.shape[0] // 2
    both = in_ref[...]
    incoming = dot(pick(rows, capacity, 0), both, 1, 0).astype(BF16)
    pre_gate = dot(incoming, gate_ref[0], 1, 0)
    pre_up = dot(incoming, up_ref[0], 1, 0)
    expert_grad = dot(pick(rows, capacity, 1), both, 1, 0).astype(BF16)
    sigma = jax.nn.sigmoid(pre_gate)
    activated = pre_gate * sigma
    slope = sigma * (1.0 + pre_gate * (1.0 - sigma))
    hidden = (activated * pre_up).astype(BF16)
    grad_hidden = dot(expert_grad, down_ref[0], 1, 1)
    dgate = (grad_hidden * pre_up * slope).astype(BF16)
    dup = (grad_hidden * activated).astype(BF16)
    units = hidden.shape[1]
    for k, factor in enumerate((dgate, dup, hidden)):
        factors_ref[:, k * units : (k + 1) * units] = factor
    stores = [pltpu.make_async_copy(factors_ref, factors_hbm, sems.at[3])]
    stores[0].start()
    for k, (factor, operand) in enumerate(
        ((dgate, incoming), (dup, incoming), (hidden, expert_grad))
    ):
        term = dot(factor, operand, 0, 0).astype(BF16)
        terms_ref[:, k] = term.reshape(parts, term.shape[0] // parts, term.shape[1])
        stores.append(pltpu.make_async_copy(terms_ref.at[:, k], terms_hbm.at[:, k], sems.at[k]))
        stores[-1].start()
    for store in stores:
        store.wait()


def returns_kernel(
    capacity, factors_hbm, gate_ref, up_ref, down_hbm, out_ref, factors_ref, down_ref, sems
):
    loads = (
        pltpu.make_async_copy(factors_hbm, factors_ref, sems.at[0]),
        pltpu.make_async_copy(down_hbm, down_ref, sems.at[1]),
    )
    for load in loads:
        load.start()
    for load in loads:
        load.wait()
    rows, units = factors_ref.shape[0], gate_ref.shape[2]
    dgate, dup, hidden = (factors_ref[:, k * units : (k + 1) * units] for k in range(3))
    back = dot(hidden, down_ref[0], 1, 0).astype(BF16)
    grad = (
        dot(dgate, gate_ref[0], 1, 1) + dot(dup, up_ref[0], 1, 1)
    ).astype(BF16)
    out = dot(pick(rows, capacity, 0), back, 0, 0) + dot(pick(rows, capacity, 1), grad, 0, 0)
    out_ref[...] = out.astype(BF16)


def combine_kernel(
    experts, capacity, ids_ref, gates_ref, grad_ref, back_ref, out_ref, dtok_ref, dgates_ref
):
    target = slots_of(ids_ref[...], experts, capacity)
    gates = column_of(gates_ref[...])
    rows = 2 * capacity * experts
    back = back_ref[...]
    slot_out = dot(hot(target, rows), back, 0, 0)
    dtok_ref[...] = dot(hot(target + capacity, rows), back, 0, 0).astype(BF16)
    out_ref[...] = (gates * slot_out).astype(BF16)
    value = jnp.sum(grad_ref[...].astype(F32) * slot_out, axis=1, keepdims=True)
    tok = value.shape[0]
    eye = iota((tok, tok), 0) == iota((tok, tok), 1)
    dgates_ref[...] = jnp.sum(jnp.where(eye, value, 0.0), axis=0, keepdims=True)


def split_kernel(in_hbm, *refs):
    outs, sems = refs[:3], refs[3]
    part = in_hbm.shape[0] // 3
    copies = [
        pltpu.make_async_copy(in_hbm.at[pl.ds(k * part, part)], out.at[0], sems.at[k])
        for k, out in enumerate(outs)
    ]
    for copy in copies:
        copy.start()
    for copy in copies:
        copy.wait()


def call(kernel, out_shape, in_specs, out_specs, scratch, vmem_mib, flops, traffic, name):
    return pl.pallas_call(
        kernel,
        out_shape=out_shape,
        in_specs=in_specs,
        out_specs=out_specs,
        scratch_shapes=scratch,
        compiler_params=pltpu.CompilerParams(vmem_limit_bytes=vmem_mib * 2**20),
        cost_estimate=pl.CostEstimate(flops=flops, bytes_accessed=traffic, transcendentals=0),
        name=name,
    )


def in_hbm(*arrays):
    return [pltpu.with_memory_space_constraint(a, pltpu.HBM) for a in arrays]


def move_rows(buffer):
    return lax.all_to_all(buffer, ("node", "local"), split_axis=0, concat_axis=0, tiled=True)


def on_device(tokens, expert_ids, gates, out_grad, w_gate, w_up, w_down):
    experts = lax.axis_size("node") * lax.axis_size("local")
    parts = lax.axis_size("dp")
    tok, width = tokens.shape
    units = w_gate.shape[2]
    capacity = max(2, 2 * tok // experts)
    rows = experts * capacity
    sds = jax.ShapeDtypeStruct
    ids = expert_ids.reshape(1, tok)
    gate_row = gates.reshape(1, tok)
    dma = pltpu.SemaphoreType.DMA
    outgoing = call(
        functools.partial(dispatch_kernel, experts, capacity),
        sds((2 * rows, width), BF16), [HBM] * 4, VMEM,
        [pltpu.VMEM((1, tok), jnp.int32), pltpu.VMEM((1, tok), F32)]
        + [pltpu.VMEM((tok, width), BF16)] * 2 + [dma((4,))],
        12, 8 * rows * tok * width, 8 * tok * width, "dispatch",
    )(*in_hbm(ids, gate_row, tokens, out_grad))
    incoming = move_rows(outgoing.reshape(experts, 2 * capacity, width)).reshape(2 * rows, width)
    blocks = (parts, 3, units // parts, width)
    terms, factors = call(
        functools.partial(terms_kernel, capacity, parts),
        (pltpu.HBM(blocks, BF16), pltpu.HBM((rows, 3 * units), BF16)), [VMEM] * 4, [HBM] * 2,
        [pltpu.VMEM(blocks, BF16), pltpu.VMEM((rows, 3 * units), BF16), dma((4,))],
        20, 18 * rows * width * units, 10 * width * units + 4 * rows * width, "terms",
    )(incoming, w_gate, w_up, w_down)
    shares = lax.psum_scatter(
        terms.reshape(3 * units, width), "dp", scatter_dimension=0, tiled=True
    )
    back = call(
        functools.partial(returns_kernel, capacity),
        sds((2 * rows, width), BF16), [HBM, VMEM, VMEM, HBM], VMEM,
        [pltpu.VMEM((rows, 3 * units), BF16), pltpu.VMEM((1, units, width), BF16), dma((2,))], 16,
        10 * rows * width * units, 6 * width * units + 4 * rows * width, "returns",
    )(*in_hbm(factors), w_gate, w_up, *in_hbm(w_down))
    back = move_rows(back.reshape(experts, 2 * capacity, width)).reshape(2 * rows, width)
    layer_out, grad_in, grad_gates = call(
        functools.partial(combine_kernel, experts, capacity),
        (sds((tok, width), BF16), sds((tok, width), BF16), sds((1, tok), F32)),
        [VMEM] * 4, [VMEM] * 3, [], 12, 8 * rows * tok * width, 10 * tok * width, "combine",
    )(ids, gate_row, out_grad, back)
    share = pltpu.HBM((1, units // parts, width), BF16)
    grads = call(
        split_kernel, (share,) * 3, [HBM], [HBM] * 3, [dma((3,))], 4, 0, 2 * 3 * units // parts * width, "split"
    )(*in_hbm(shares))
    return (layer_out, grad_in, grad_gates.reshape(tok, 1), *grads)


def solution(mesh):
    by_token = P(("dp", "node", "local"), None)
    by_expert = P(("node", "local"), None, None)
    by_share = P(("node", "local"), "dp", None)
    return jax.shard_map(
        on_device,
        mesh=mesh,
        in_specs=(by_token,) * 4 + (by_expert,) * 3,
        out_specs=(by_token,) * 3 + (by_share,) * 3,
        check_vma=False,
    )
```

```python
import functools

import jax
import jax.numpy as jnp
from jax import lax
from jax.experimental import pallas as pl
from jax.experimental.pallas import tpu as pltpu
from jax.sharding import PartitionSpec as P

BF16 = jnp.bfloat16
F32 = jnp.float32
COLS = 4
VMEM = pl.BlockSpec(memory_space=pltpu.VMEM)
HBM = pl.BlockSpec(memory_space=pltpu.HBM)


def dot(a, b, da, db):
    return lax.dot_general(a, b, (((da,), (db,)), ((), ())), preferred_element_type=F32)


def iota(shape, dim):
    return lax.broadcasted_iota(jnp.int32, shape, dim)


def slots_of(ids, experts, capacity):
    tok = ids.shape[1]
    named = iota((experts, tok), 0) == ids
    before = (iota((tok, tok), 0) < iota((tok, tok), 1)).astype(BF16)
    rank = dot(named.astype(BF16), before, 1, 0)
    place = jnp.sum(jnp.where(named, rank, 0.0), axis=0, keepdims=True).astype(jnp.int32)
    return ids * (2 * capacity) + place


def column_of(row):
    tok = row.shape[1]
    eye = iota((tok, tok), 0) == iota((tok, tok), 1)
    return jnp.sum(jnp.where(eye, row, 0.0), axis=1, keepdims=True)


def hot(target, rows):
    return (iota((rows, target.shape[1]), 0) == target).astype(F32).astype(BF16)


def dispatch_kernel(
    experts, capacity, ids_hbm, gates_hbm, tokens_hbm, grad_hbm, out_ref,
    ids_ref, gates_ref, tokens_ref, grad_ref, sems,
):
    loads = [
        pltpu.make_async_copy(src, dst, sems.at[i])
        for i, (src, dst) in enumerate((
            (ids_hbm, ids_ref), (gates_hbm, gates_ref), (tokens_hbm, tokens_ref), (grad_hbm, grad_ref)
        ))
    ]
    for load in loads:
        load.start()
    loads[0].wait()
    target = slots_of(ids_ref[...], experts, capacity)
    rows = 2 * capacity * experts
    to_token, to_grad = hot(target, rows), hot(target + capacity, rows)
    loads[1].wait()
    gates = column_of(gates_ref[...])
    loads[2].wait()
    out = dot(to_token, tokens_ref[...], 1, 0)
    loads[3].wait()
    scaled = (gates * grad_ref[...].astype(F32)).astype(BF16)
    out += dot(to_grad, scaled, 1, 0)
    out_ref[...] = out.astype(BF16)


def pick(rows, capacity, kind):
    at, of = iota((rows, 2 * rows), 0), iota((rows, 2 * rows), 1)
    return (of == at + (at // capacity + kind) * capacity).astype(F32).astype(BF16)


def terms_kernel(
    capacity, parts, in_ref, gate_ref, up_ref, down_ref, terms_hbm, factors_hbm,
    terms_ref, factors_ref, sems,
):
    rows, width = in_ref.shape[0] // 2, in_ref.shape[1]
    both = in_ref[...].reshape(rows // capacity, 2 * capacity, width)
    incoming = both[:, :capacity].reshape(rows, width)
    expert_grad = both[:, capacity:].reshape(rows, width)
    pre_gate = dot(incoming, gate_ref[0], 1, 0)
    pre_up = dot(incoming, up_ref[0], 1, 0)
    sigma = jax.nn.sigmoid(pre_gate)
    activated = pre_gate * sigma
    slope = sigma * (1.0 + pre_gate * (1.0 - sigma))
    hidden = (activated * pre_up).astype(BF16)
    grad_hidden = dot(expert_grad, down_ref[0], 1, 1)
    dgate = (grad_hidden * pre_up * slope).astype(BF16)
    dup = (grad_hidden * activated).astype(BF16)
    units = hidden.shape[1]
    for k, factor in enumerate((dgate, dup, hidden)):
        factors_ref[:, k * units : (k + 1) * units] = factor
    stores = [pltpu.make_async_copy(factors_ref, factors_hbm, sems.at[0])]
    stores[0].start()
    step = width // COLS
    for k, (factor, operand) in enumerate(
        ((dgate, incoming), (dup, incoming), (hidden, expert_grad))
    ):
        for h in range(COLS):
            cols = pl.ds(h * step, step)
            term = dot(factor, operand[:, h * step : (h + 1) * step], 0, 0).astype(BF16)
            terms_ref[:, k, :, cols] = term.reshape(parts, units // parts, step)
            stores.append(
                pltpu.make_async_copy(
                    terms_ref.at[:, k, :, cols], terms_hbm.at[:, k, :, cols],
                    sems.at[len(stores)],
                )
            )
            stores[-1].start()
    for store in stores:
        store.wait()


def returns_kernel(
    capacity, factors_hbm, gate_ref, up_ref, down_hbm, out_ref, factors_ref, down_ref, sems
):
    loads = (
        pltpu.make_async_copy(factors_hbm, factors_ref, sems.at[0]),
        pltpu.make_async_copy(down_hbm, down_ref, sems.at[1]),
    )
    for load in loads:
        load.start()
    for load in loads:
        load.wait()
    rows, units = factors_ref.shape[0], gate_ref.shape[2]
    dgate, dup, hidden = (factors_ref[:, k * units : (k + 1) * units] for k in range(3))
    back = dot(hidden, down_ref[0], 1, 0).astype(BF16)
    grad = (
        dot(dgate, gate_ref[0], 1, 1) + dot(dup, up_ref[0], 1, 1)
    ).astype(BF16)
    out = dot(pick(rows, capacity, 0), back, 0, 0) + dot(pick(rows, capacity, 1), grad, 0, 0)
    out_ref[...] = out.astype(BF16)


def combine_kernel(
    experts, capacity, ids_ref, gates_ref, grad_ref, back_ref, out_ref, dtok_ref, dgates_ref
):
    target = slots_of(ids_ref[...], experts, capacity)
    gates = column_of(gates_ref[...])
    rows = 2 * capacity * experts
    back = back_ref[...]
    slot_out = dot(hot(target, rows), back, 0, 0)
    dtok_ref[...] = dot(hot(target + capacity, rows), back, 0, 0).astype(BF16)
    out_ref[...] = (gates * slot_out).astype(BF16)
    value = jnp.sum(grad_ref[...].astype(F32) * slot_out, axis=1, keepdims=True)
    tok = value.shape[0]
    eye = iota((tok, tok), 0) == iota((tok, tok), 1)
    dgates_ref[...] = jnp.sum(jnp.where(eye, value, 0.0), axis=0, keepdims=True)


def split_kernel(in_hbm, *refs):
    outs, held, sems = refs[:3], refs[3], refs[4]
    part = in_hbm.shape[0] // 3
    loads = [
        pltpu.make_async_copy(in_hbm.at[pl.ds(k * part, part)], held.at[k], sems.at[k])
        for k in range(3)
    ]
    stores = [pltpu.make_async_copy(held.at[k], outs[k].at[0], sems.at[3 + k]) for k in range(3)]
    for load in loads:
        load.start()
    for load, store in zip(loads, stores):
        load.wait()
        store.start()
    for store in stores:
        store.wait()


def call(kernel, out_shape, in_specs, out_specs, scratch, vmem_mib, flops, traffic, name):
    return pl.pallas_call(
        kernel,
        out_shape=out_shape,
        in_specs=in_specs,
        out_specs=out_specs,
        scratch_shapes=scratch,
        compiler_params=pltpu.CompilerParams(vmem_limit_bytes=vmem_mib * 2**20),
        cost_estimate=pl.CostEstimate(flops=flops, bytes_accessed=traffic, transcendentals=0),
        name=name,
    )


def in_hbm(*arrays):
    return [pltpu.with_memory_space_constraint(a, pltpu.HBM) for a in arrays]


def move_rows(buffer):
    return lax.all_to_all(buffer, ("node", "local"), split_axis=0, concat_axis=0, tiled=True)


def on_device(tokens, expert_ids, gates, out_grad, w_gate, w_up, w_down):
    experts = lax.axis_size("node") * lax.axis_size("local")
    parts = lax.axis_size("dp")
    tok, width = tokens.shape
    units = w_gate.shape[2]
    capacity = max(2, 2 * tok // experts)
    rows = experts * capacity
    sds = jax.ShapeDtypeStruct
    ids = expert_ids.reshape(1, tok)
    gate_row = gates.reshape(1, tok)
    dma = pltpu.SemaphoreType.DMA
    outgoing = call(
        functools.partial(dispatch_kernel, experts, capacity),
        sds((2 * rows, width), BF16), [HBM] * 4, VMEM,
        [pltpu.VMEM((1, tok), jnp.int32), pltpu.VMEM((1, tok), F32)]
        + [pltpu.VMEM((tok, width), BF16)] * 2 + [dma((4,))],
        12, 8 * rows * tok * width, 8 * tok * width, "dispatch",
    )(*in_hbm(ids, gate_row, tokens, out_grad))
    incoming = move_rows(outgoing.reshape(experts, 2 * capacity, width)).reshape(2 * rows, width)
    blocks = (parts, 3, units // parts, width)
    terms, factors = call(
        functools.partial(terms_kernel, capacity, parts),
        (pltpu.HBM(blocks, BF16), pltpu.HBM((rows, 3 * units), BF16)), [VMEM] * 4, [HBM] * 2,
        [pltpu.VMEM(blocks, BF16), pltpu.VMEM((rows, 3 * units), BF16), dma((3 * COLS + 1,))],
        20, 18 * rows * width * units, 10 * width * units + 4 * rows * width, "terms",
    )(incoming, w_gate, w_up, w_down)
    shares = lax.psum_scatter(
        terms.reshape(3 * units, width), "dp", scatter_dimension=0, tiled=True
    )
    back = call(
        functools.partial(returns_kernel, capacity),
        sds((2 * rows, width), BF16), [HBM, VMEM, VMEM, HBM], VMEM,
        [pltpu.VMEM((rows, 3 * units), BF16), pltpu.VMEM((1, units, width), BF16), dma((2,))], 16,
        10 * rows * width * units, 6 * width * units + 4 * rows * width, "returns",
    )(*in_hbm(factors), w_gate, w_up, *in_hbm(w_down))
    back = move_rows(back.reshape(experts, 2 * capacity, width)).reshape(2 * rows, width)
    layer_out, grad_in, grad_gates = call(
        functools.partial(combine_kernel, experts, capacity),
        (sds((tok, width), BF16), sds((tok, width), BF16), sds((1, tok), F32)),
        [VMEM] * 4, [VMEM] * 3, [], 12, 8 * rows * tok * width, 10 * tok * width, "combine",
    )(ids, gate_row, out_grad, back)
    share = pltpu.HBM((1, units // parts, width), BF16)
    grads = call(
        split_kernel, (share,) * 3, [HBM], [HBM] * 3,
        [pltpu.VMEM((3, units // parts, width), BF16), dma((6,))], 4, 0, 2 * 3 * units // parts * width, "split"
    )(*in_hbm(shares))
    return (layer_out, grad_in, grad_gates.reshape(tok, 1), *grads)


def solution(mesh):
    by_token = P(("dp", "node", "local"), None)
    by_expert = P(("node", "local"), None, None)
    by_share = P(("node", "local"), "dp", None)
    return jax.shard_map(
        on_device,
        mesh=mesh,
        in_specs=(by_token,) * 4 + (by_expert,) * 3,
        out_specs=(by_token,) * 3 + (by_share,) * 3,
        check_vma=False,
    )
```

```python
import functools

import jax
import jax.numpy as jnp
from jax import lax
from jax.experimental import pallas as pl
from jax.experimental.pallas import tpu as pltpu
from jax.sharding import PartitionSpec as P

BF16 = jnp.bfloat16
F32 = jnp.float32
COLS = 4
VMEM = pl.BlockSpec(memory_space=pltpu.VMEM)
HBM = pl.BlockSpec(memory_space=pltpu.HBM)


def dot(a, b, da, db):
    return lax.dot_general(a, b, (((da,), (db,)), ((), ())), preferred_element_type=F32)


def iota(shape, dim):
    return lax.broadcasted_iota(jnp.int32, shape, dim)


def slots_of(ids, experts, capacity):
    tok = ids.shape[1]
    named = iota((experts, tok), 0) == ids
    before = (iota((tok, tok), 0) < iota((tok, tok), 1)).astype(BF16)
    rank = dot(named.astype(BF16), before, 1, 0)
    place = jnp.sum(jnp.where(named, rank, 0.0), axis=0, keepdims=True).astype(jnp.int32)
    return ids * (2 * capacity) + place


def column_of(row):
    tok = row.shape[1]
    eye = iota((tok, tok), 0) == iota((tok, tok), 1)
    return jnp.sum(jnp.where(eye, row, 0.0), axis=1, keepdims=True)


def hot(target, rows):
    return (iota((rows, target.shape[1]), 0) == target).astype(F32).astype(BF16)


def dispatch_kernel(
    experts, capacity, ids_hbm, gates_hbm, tokens_hbm, grad_hbm, out_ref,
    ids_ref, gates_ref, tokens_ref, grad_ref, sems,
):
    loads = [
        pltpu.make_async_copy(src, dst, sems.at[i])
        for i, (src, dst) in enumerate((
            (ids_hbm, ids_ref), (gates_hbm, gates_ref), (tokens_hbm, tokens_ref), (grad_hbm, grad_ref)
        ))
    ]
    for load in loads:
        load.start()
    loads[0].wait()
    target = slots_of(ids_ref[...], experts, capacity)
    rows = 2 * capacity * experts
    place = jnp.concatenate([hot(target, rows), hot(target + capacity, rows)], axis=1)
    loads[1].wait()
    gates = column_of(gates_ref[...])
    loads[2].wait()
    loads[3].wait()
    scaled = (gates * grad_ref[...].astype(F32)).astype(BF16)
    both = jnp.concatenate([tokens_ref[...], scaled], axis=0)
    out_ref[...] = dot(place, both, 1, 0).astype(BF16)


def pick(rows, capacity, kind):
    at, of = iota((rows, 2 * rows), 0), iota((rows, 2 * rows), 1)
    return (of == at + (at // capacity + kind) * capacity).astype(F32).astype(BF16)


def terms_kernel(
    capacity, parts, in_ref, gate_ref, up_ref, down_ref, terms_hbm, factors_hbm,
    terms_ref, factors_ref, sems,
):
    rows, width = in_ref.shape[0] // 2, in_ref.shape[1]
    both = in_ref[...].reshape(rows // capacity, 2 * capacity, width)
    incoming = both[:, :capacity].reshape(rows, width)
    expert_grad = both[:, capacity:].reshape(rows, width)
    pre_gate = dot(incoming, gate_ref[0], 1, 0)
    pre_up = dot(incoming, up_ref[0], 1, 0)
    sigma = jax.nn.sigmoid(pre_gate)
    activated = pre_gate * sigma
    slope = sigma * (1.0 + pre_gate * (1.0 - sigma))
    hidden = (activated * pre_up).astype(BF16)
    grad_hidden = dot(expert_grad, down_ref[0], 1, 1)
    dgate = (grad_hidden * pre_up * slope).astype(BF16)
    dup = (grad_hidden * activated).astype(BF16)
    units = hidden.shape[1]
    for k, factor in enumerate((dgate, dup, hidden)):
        factors_ref[:, k * units : (k + 1) * units] = factor
    stores = [pltpu.make_async_copy(factors_ref, factors_hbm, sems.at[0])]
    stores[0].start()
    step = width // COLS
    for k, (factor, operand) in enumerate(
        ((dgate, incoming), (dup, incoming), (hidden, expert_grad))
    ):
        for h in range(COLS):
            cols = pl.ds(h * step, step)
            term = dot(factor, operand[:, h * step : (h + 1) * step], 0, 0).astype(BF16)
            terms_ref[:, k, :, cols] = term.reshape(parts, units // parts, step)
            stores.append(
                pltpu.make_async_copy(
                    terms_ref.at[:, k, :, cols], terms_hbm.at[:, k, :, cols],
                    sems.at[len(stores)],
                )
            )
            stores[-1].start()
    for store in stores:
        store.wait()


def returns_kernel(
    capacity, factors_hbm, gate_ref, up_ref, down_hbm, out_ref, factors_ref, down_ref, sems
):
    loads = (
        pltpu.make_async_copy(factors_hbm, factors_ref, sems.at[0]),
        pltpu.make_async_copy(down_hbm, down_ref, sems.at[1]),
    )
    for load in loads:
        load.start()
    for load in loads:
        load.wait()
    rows, units = factors_ref.shape[0], gate_ref.shape[2]
    dgate, dup, hidden = (factors_ref[:, k * units : (k + 1) * units] for k in range(3))
    back = dot(hidden, down_ref[0], 1, 0).astype(BF16)
    grad = (
        dot(dgate, gate_ref[0], 1, 1) + dot(dup, up_ref[0], 1, 1)
    ).astype(BF16)
    out = dot(pick(rows, capacity, 0), back, 0, 0) + dot(pick(rows, capacity, 1), grad, 0, 0)
    out_ref[...] = out.astype(BF16)


def combine_kernel(
    experts, capacity, ids_ref, gates_ref, grad_ref, back_ref, out_ref, dtok_ref, dgates_ref
):
    target = slots_of(ids_ref[...], experts, capacity)
    gates = column_of(gates_ref[...])
    rows = 2 * capacity * experts
    back = back_ref[...]
    slot_out = dot(hot(target, rows), back, 0, 0)
    dtok_ref[...] = dot(hot(target + capacity, rows), back, 0, 0).astype(BF16)
    out_ref[...] = (gates * slot_out).astype(BF16)
    value = jnp.sum(grad_ref[...].astype(F32) * slot_out, axis=1, keepdims=True)
    tok = value.shape[0]
    eye = iota((tok, tok), 0) == iota((tok, tok), 1)
    dgates_ref[...] = jnp.sum(jnp.where(eye, value, 0.0), axis=0, keepdims=True)


def split_kernel(in_hbm, *refs):
    outs, held, sems = refs[:3], refs[3], refs[4]
    part = in_hbm.shape[0] // 3
    loads = [
        pltpu.make_async_copy(in_hbm.at[pl.ds(k * part, part)], held.at[k], sems.at[k])
        for k in range(3)
    ]
    stores = [pltpu.make_async_copy(held.at[k], outs[k].at[0], sems.at[3 + k]) for k in range(3)]
    for load in loads:
        load.start()
    for load, store in zip(loads, stores):
        load.wait()
        store.start()
    for store in stores:
        store.wait()


def call(kernel, out_shape, in_specs, out_specs, scratch, vmem_mib, flops, traffic, name):
    return pl.pallas_call(
        kernel,
        out_shape=out_shape,
        in_specs=in_specs,
        out_specs=out_specs,
        scratch_shapes=scratch,
        compiler_params=pltpu.CompilerParams(vmem_limit_bytes=vmem_mib * 2**20),
        cost_estimate=pl.CostEstimate(flops=flops, bytes_accessed=traffic, transcendentals=0),
        name=name,
    )


def in_hbm(*arrays):
    return [pltpu.with_memory_space_constraint(a, pltpu.HBM) for a in arrays]


def move_rows(buffer):
    return lax.all_to_all(buffer, ("node", "local"), split_axis=0, concat_axis=0, tiled=True)


def on_device(tokens, expert_ids, gates, out_grad, w_gate, w_up, w_down):
    experts = lax.axis_size("node") * lax.axis_size("local")
    parts = lax.axis_size("dp")
    tok, width = tokens.shape
    units = w_gate.shape[2]
    capacity = max(2, 2 * tok // experts)
    rows = experts * capacity
    sds = jax.ShapeDtypeStruct
    ids = expert_ids.reshape(1, tok)
    gate_row = gates.reshape(1, tok)
    dma = pltpu.SemaphoreType.DMA
    outgoing = call(
        functools.partial(dispatch_kernel, experts, capacity),
        sds((2 * rows, width), BF16), [HBM] * 4, VMEM,
        [pltpu.VMEM((1, tok), jnp.int32), pltpu.VMEM((1, tok), F32)]
        + [pltpu.VMEM((tok, width), BF16)] * 2 + [dma((4,))],
        12, 8 * rows * tok * width, 8 * tok * width, "dispatch",
    )(*in_hbm(ids, gate_row, tokens, out_grad))
    incoming = move_rows(outgoing.reshape(experts, 2 * capacity, width)).reshape(2 * rows, width)
    blocks = (parts, 3, units // parts, width)
    terms, factors = call(
        functools.partial(terms_kernel, capacity, parts),
        (pltpu.HBM(blocks, BF16), pltpu.HBM((rows, 3 * units), BF16)), [VMEM] * 4, [HBM] * 2,
        [pltpu.VMEM(blocks, BF16), pltpu.VMEM((rows, 3 * units), BF16), dma((3 * COLS + 1,))],
        20, 18 * rows * width * units, 10 * width * units + 4 * rows * width, "terms",
    )(incoming, w_gate, w_up, w_down)
    shares = lax.psum_scatter(
        terms.reshape(3 * units, width), "dp", scatter_dimension=0, tiled=True
    )
    back = call(
        functools.partial(returns_kernel, capacity),
        sds((2 * rows, width), BF16), [HBM, VMEM, VMEM, HBM], VMEM,
        [pltpu.VMEM((rows, 3 * units), BF16), pltpu.VMEM((1, units, width), BF16), dma((2,))], 16,
        10 * rows * width * units, 6 * width * units + 4 * rows * width, "returns",
    )(*in_hbm(factors), w_gate, w_up, *in_hbm(w_down))
    back = move_rows(back.reshape(experts, 2 * capacity, width)).reshape(2 * rows, width)
    layer_out, grad_in, grad_gates = call(
        functools.partial(combine_kernel, experts, capacity),
        (sds((tok, width), BF16), sds((tok, width), BF16), sds((1, tok), F32)),
        [VMEM] * 4, [VMEM] * 3, [], 12, 8 * rows * tok * width, 10 * tok * width, "combine",
    )(ids, gate_row, out_grad, back)
    share = pltpu.HBM((1, units // parts, width), BF16)
    grads = call(
        split_kernel, (share,) * 3, [HBM], [HBM] * 3,
        [pltpu.VMEM((3, units // parts, width), BF16), dma((6,))], 4, 0, 2 * 3 * units // parts * width, "split"
    )(*in_hbm(shares))
    return (layer_out, grad_in, grad_gates.reshape(tok, 1), *grads)


def solution(mesh):
    by_token = P(("dp", "node", "local"), None)
    by_expert = P(("node", "local"), None, None)
    by_share = P(("node", "local"), "dp", None)
    return jax.shard_map(
        on_device,
        mesh=mesh,
        in_specs=(by_token,) * 4 + (by_expert,) * 3,
        out_specs=(by_token,) * 3 + (by_share,) * 3,
        check_vma=False,
    )
```

```python
import functools

import jax
import jax.numpy as jnp
from jax import lax
from jax.experimental import pallas as pl
from jax.experimental.pallas import tpu as pltpu
from jax.sharding import PartitionSpec as P

BF16 = jnp.bfloat16
F32 = jnp.float32
COLS = 4
VMEM = pl.BlockSpec(memory_space=pltpu.VMEM)
HBM = pl.BlockSpec(memory_space=pltpu.HBM)


def dot(a, b, da, db):
    return lax.dot_general(a, b, (((da,), (db,)), ((), ())), preferred_element_type=F32)


def iota(shape, dim):
    return lax.broadcasted_iota(jnp.int32, shape, dim)


def slots_of(ids, experts, capacity):
    tok = ids.shape[1]
    named = iota((experts, tok), 0) == ids
    before = (iota((tok, tok), 0) < iota((tok, tok), 1)).astype(BF16)
    rank = dot(named.astype(BF16), before, 1, 0)
    place = jnp.sum(jnp.where(named, rank, 0.0), axis=0, keepdims=True).astype(jnp.int32)
    return ids * (2 * capacity) + place


def column_of(row):
    tok = row.shape[1]
    eye = iota((tok, tok), 0) == iota((tok, tok), 1)
    return jnp.sum(jnp.where(eye, row, 0.0), axis=1, keepdims=True)


def hot(target, rows):
    return (iota((rows, target.shape[1]), 0) == target).astype(F32).astype(BF16)


def dispatch_kernel(
    experts, capacity, ids_hbm, gates_hbm, tokens_hbm, grad_hbm, out_ref,
    ids_ref, gates_ref, tokens_ref, grad_ref, sems,
):
    loads = [
        pltpu.make_async_copy(src, dst, sems.at[i])
        for i, (src, dst) in enumerate((
            (ids_hbm, ids_ref), (gates_hbm, gates_ref), (tokens_hbm, tokens_ref), (grad_hbm, grad_ref)
        ))
    ]
    for load in loads:
        load.start()
    loads[0].wait()
    target = slots_of(ids_ref[...], experts, capacity)
    rows = 2 * capacity * experts
    place = jnp.concatenate([hot(target, rows), hot(target + capacity, rows)], axis=1)
    loads[1].wait()
    gates = column_of(gates_ref[...])
    loads[2].wait()
    loads[3].wait()
    scaled = (gates * grad_ref[...].astype(F32)).astype(BF16)
    both = jnp.concatenate([tokens_ref[...], scaled], axis=0)
    out_ref[...] = dot(place, both, 1, 0).astype(BF16)


def terms_kernel(
    capacity, parts, in_ref, gate_ref, up_ref, down_ref, terms_hbm, factors_hbm,
    terms_ref, factors_ref, sems,
):
    rows, width = in_ref.shape[0] // 2, in_ref.shape[1]
    both = in_ref[...].reshape(rows // capacity, 2 * capacity, width)
    incoming = both[:, :capacity].reshape(rows, width)
    expert_grad = both[:, capacity:].reshape(rows, width)
    pre_gate = dot(incoming, gate_ref[0], 1, 0)
    pre_up = dot(incoming, up_ref[0], 1, 0)
    sigma = jax.nn.sigmoid(pre_gate)
    activated = pre_gate * sigma
    slope = sigma * (1.0 + pre_gate * (1.0 - sigma))
    hidden = (activated * pre_up).astype(BF16)
    grad_hidden = dot(expert_grad, down_ref[0], 1, 1)
    dgate = (grad_hidden * pre_up * slope).astype(BF16)
    dup = (grad_hidden * activated).astype(BF16)
    units = hidden.shape[1]
    for k, factor in enumerate((dgate, dup, hidden)):
        factors_ref[:, k * units : (k + 1) * units] = factor
    stores = [pltpu.make_async_copy(factors_ref, factors_hbm, sems.at[0])]
    stores[0].start()
    step = width // COLS
    for k, (factor, operand) in enumerate(
        ((dgate, incoming), (dup, incoming), (hidden, expert_grad))
    ):
        for h in range(COLS):
            cols = pl.ds(h * step, step)
            term = dot(factor, operand[:, h * step : (h + 1) * step], 0, 0).astype(BF16)
            terms_ref[:, k, :, cols] = term.reshape(parts, units // parts, step)
            stores.append(
                pltpu.make_async_copy(
                    terms_ref.at[:, k, :, cols], terms_hbm.at[:, k, :, cols],
                    sems.at[len(stores)],
                )
            )
            stores[-1].start()
    for store in stores:
        store.wait()


def returns_kernel(
    capacity, factors_hbm, gate_ref, up_ref, down_hbm, out_ref, factors_ref, down_ref, sems
):
    loads = (
        pltpu.make_async_copy(factors_hbm, factors_ref, sems.at[0]),
        pltpu.make_async_copy(down_hbm, down_ref, sems.at[1]),
    )
    for load in loads:
        load.start()
    rows, units, width = factors_ref.shape[0], gate_ref.shape[2], out_ref.shape[1]
    loads[0].wait()
    dgate, dup, hidden = (factors_ref[:, k * units : (k + 1) * units] for k in range(3))
    grad = dot(dgate, gate_ref[0], 1, 1) + dot(dup, up_ref[0], 1, 1)
    loads[1].wait()
    back = dot(hidden, down_ref[0], 1, 0)
    groups = (rows // capacity, capacity, width)
    both = [x.astype(BF16).reshape(groups) for x in (back, grad)]
    out_ref[...] = jnp.concatenate(both, axis=1).reshape(2 * rows, width)


def combine_kernel(
    experts, capacity, ids_ref, gates_ref, grad_ref, back_ref, out_ref, dtok_ref, dgates_ref
):
    target = slots_of(ids_ref[...], experts, capacity)
    gates = column_of(gates_ref[...])
    rows = 2 * capacity * experts
    back = back_ref[...]
    slot_out = dot(hot(target, rows), back, 0, 0)
    dtok_ref[...] = dot(hot(target + capacity, rows), back, 0, 0).astype(BF16)
    out_ref[...] = (gates * slot_out).astype(BF16)
    value = jnp.sum(grad_ref[...].astype(F32) * slot_out, axis=1, keepdims=True)
    tok = value.shape[0]
    eye = iota((tok, tok), 0) == iota((tok, tok), 1)
    dgates_ref[...] = jnp.sum(jnp.where(eye, value, 0.0), axis=0, keepdims=True)


def split_kernel(in_hbm, *refs):
    outs, held, sems = refs[:3], refs[3], refs[4]
    part = in_hbm.shape[0] // 3
    loads = [
        pltpu.make_async_copy(in_hbm.at[pl.ds(k * part, part)], held.at[k], sems.at[k])
        for k in range(3)
    ]
    stores = [pltpu.make_async_copy(held.at[k], outs[k].at[0], sems.at[3 + k]) for k in range(3)]
    for load in loads:
        load.start()
    for load, store in zip(loads, stores):
        load.wait()
        store.start()
    for store in stores:
        store.wait()


def call(kernel, out_shape, in_specs, out_specs, scratch, vmem_mib, flops, traffic, name):
    return pl.pallas_call(
        kernel,
        out_shape=out_shape,
        in_specs=in_specs,
        out_specs=out_specs,
        scratch_shapes=scratch,
        compiler_params=pltpu.CompilerParams(vmem_limit_bytes=vmem_mib * 2**20),
        cost_estimate=pl.CostEstimate(flops=flops, bytes_accessed=traffic, transcendentals=0),
        name=name,
    )


def in_hbm(*arrays):
    return [pltpu.with_memory_space_constraint(a, pltpu.HBM) for a in arrays]


def move_rows(buffer):
    return lax.all_to_all(buffer, ("node", "local"), split_axis=0, concat_axis=0, tiled=True)


def on_device(tokens, expert_ids, gates, out_grad, w_gate, w_up, w_down):
    experts = lax.axis_size("node") * lax.axis_size("local")
    parts = lax.axis_size("dp")
    tok, width = tokens.shape
    units = w_gate.shape[2]
    capacity = max(2, 2 * tok // experts)
    rows = experts * capacity
    sds = jax.ShapeDtypeStruct
    ids = expert_ids.reshape(1, tok)
    gate_row = gates.reshape(1, tok)
    dma = pltpu.SemaphoreType.DMA
    outgoing = call(
        functools.partial(dispatch_kernel, experts, capacity),
        sds((2 * rows, width), BF16), [HBM] * 4, VMEM,
        [pltpu.VMEM((1, tok), jnp.int32), pltpu.VMEM((1, tok), F32)]
        + [pltpu.VMEM((tok, width), BF16)] * 2 + [dma((4,))],
        12, 8 * rows * tok * width, 8 * tok * width, "dispatch",
    )(*in_hbm(ids, gate_row, tokens, out_grad))
    incoming = move_rows(outgoing.reshape(experts, 2 * capacity, width)).reshape(2 * rows, width)
    blocks = (parts, 3, units // parts, width)
    terms, factors = call(
        functools.partial(terms_kernel, capacity, parts),
        (pltpu.HBM(blocks, BF16), pltpu.HBM((rows, 3 * units), BF16)), [VMEM] * 4, [HBM] * 2,
        [pltpu.VMEM(blocks, BF16), pltpu.VMEM((rows, 3 * units), BF16), dma((3 * COLS + 1,))],
        20, 18 * rows * width * units, 10 * width * units + 4 * rows * width, "terms",
    )(incoming, w_gate, w_up, w_down)
    shares = lax.psum_scatter(
        terms.reshape(3 * units, width), "dp", scatter_dimension=0, tiled=True
    )
    back = call(
        functools.partial(returns_kernel, capacity),
        sds((2 * rows, width), BF16), [HBM, VMEM, VMEM, HBM], VMEM,
        [pltpu.VMEM((rows, 3 * units), BF16), pltpu.VMEM((1, units, width), BF16), dma((2,))], 16,
        10 * rows * width * units, 6 * width * units + 4 * rows * width, "returns",
    )(*in_hbm(factors), w_gate, w_up, *in_hbm(w_down))
    back = move_rows(back.reshape(experts, 2 * capacity, width)).reshape(2 * rows, width)
    layer_out, grad_in, grad_gates = call(
        functools.partial(combine_kernel, experts, capacity),
        (sds((tok, width), BF16), sds((tok, width), BF16), sds((1, tok), F32)),
        [VMEM] * 4, [VMEM] * 3, [], 12, 8 * rows * tok * width, 10 * tok * width, "combine",
    )(ids, gate_row, out_grad, back)
    share = pltpu.HBM((1, units // parts, width), BF16)
    grads = call(
        split_kernel, (share,) * 3, [HBM], [HBM] * 3,
        [pltpu.VMEM((3, units // parts, width), BF16), dma((6,))], 4, 0, 2 * 3 * units // parts * width, "split"
    )(*in_hbm(shares))
    return (layer_out, grad_in, grad_gates.reshape(tok, 1), *grads)


def solution(mesh):
    by_token = P(("dp", "node", "local"), None)
    by_expert = P(("node", "local"), None, None)
    by_share = P(("node", "local"), "dp", None)
    return jax.shard_map(
        on_device,
        mesh=mesh,
        in_specs=(by_token,) * 4 + (by_expert,) * 3,
        out_specs=(by_token,) * 3 + (by_share,) * 3,
        check_vma=False,
    )
```

```python
import functools

import jax
import jax.numpy as jnp
from jax import lax
from jax.experimental import pallas as pl
from jax.experimental.pallas import tpu as pltpu
from jax.sharding import PartitionSpec as P

BF16 = jnp.bfloat16
F32 = jnp.float32
COLS = 4
VMEM = pl.BlockSpec(memory_space=pltpu.VMEM)
HBM = pl.BlockSpec(memory_space=pltpu.HBM)


def dot(a, b, da, db):
    return lax.dot_general(a, b, (((da,), (db,)), ((), ())), preferred_element_type=F32)


def iota(shape, dim):
    return lax.broadcasted_iota(jnp.int32, shape, dim)


def slots_of(ids, experts, capacity):
    tok = ids.shape[1]
    named = iota((experts, tok), 0) == ids
    before = (iota((tok, tok), 0) < iota((tok, tok), 1)).astype(BF16)
    rank = dot(named.astype(BF16), before, 1, 0)
    place = jnp.sum(jnp.where(named, rank, 0.0), axis=0, keepdims=True).astype(jnp.int32)
    return ids * (2 * capacity) + place


def column_of(row):
    tok = row.shape[1]
    eye = iota((tok, tok), 0) == iota((tok, tok), 1)
    return jnp.sum(jnp.where(eye, row, 0.0), axis=1, keepdims=True)


def hot(target, rows):
    return (iota((rows, target.shape[1]), 0) == target).astype(F32).astype(BF16)


def dispatch_kernel(
    experts, capacity, ids_hbm, gates_hbm, tokens_hbm, grad_hbm, out_ref,
    ids_ref, gates_ref, tokens_ref, grad_ref, sems,
):
    loads = [
        pltpu.make_async_copy(src, dst, sems.at[i])
        for i, (src, dst) in enumerate((
            (ids_hbm, ids_ref), (gates_hbm, gates_ref), (tokens_hbm, tokens_ref), (grad_hbm, grad_ref)
        ))
    ]
    for load in loads:
        load.start()
    loads[0].wait()
    target = slots_of(ids_ref[...], experts, capacity)
    rows = 2 * capacity * experts
    place = jnp.concatenate([hot(target, rows), hot(target + capacity, rows)], axis=1)
    loads[1].wait()
    gates = column_of(gates_ref[...])
    loads[2].wait()
    loads[3].wait()
    scaled = (gates * grad_ref[...].astype(F32)).astype(BF16)
    both = jnp.concatenate([tokens_ref[...], scaled], axis=0)
    out_ref[...] = dot(place, both, 1, 0).astype(BF16)


def terms_kernel(
    capacity, in_ref, gate_ref, up_ref, down_ref, terms_hbm, factors_hbm,
    terms_ref, factors_ref, sems,
):
    rows, width = in_ref.shape[0] // 2, in_ref.shape[1]
    both = in_ref[...].reshape(rows // capacity, 2 * capacity, width)
    incoming = both[:, :capacity].reshape(rows, width)
    expert_grad = both[:, capacity:].reshape(rows, width)
    pre_gate = dot(incoming, gate_ref[0], 1, 0)
    pre_up = dot(incoming, up_ref[0], 1, 0)
    sigma = jax.nn.sigmoid(pre_gate)
    activated = pre_gate * sigma
    slope = sigma * (1.0 + pre_gate * (1.0 - sigma))
    hidden = (activated * pre_up).astype(BF16)
    grad_hidden = dot(expert_grad, down_ref[0], 1, 1)
    dgate = (grad_hidden * pre_up * slope).astype(BF16)
    dup = (grad_hidden * activated).astype(BF16)
    units = hidden.shape[1]
    for k, factor in enumerate((dgate, dup, hidden)):
        factors_ref[:, k * units : (k + 1) * units] = factor
    stores = [pltpu.make_async_copy(factors_ref, factors_hbm, sems.at[0])]
    stores[0].start()
    step = width // COLS
    for k, (factor, operand) in enumerate(
        ((dgate, incoming), (dup, incoming), (hidden, expert_grad))
    ):
        for h in range(COLS):
            cols = pl.ds(h * step, step)
            term = dot(factor, operand[:, h * step : (h + 1) * step], 0, 0).astype(BF16)
            terms_ref[k, :, cols] = term
            stores.append(
                pltpu.make_async_copy(
                    terms_ref.at[k, :, cols], terms_hbm.at[k, :, cols],
                    sems.at[len(stores)],
                )
            )
            stores[-1].start()
    for store in stores:
        store.wait()


def returns_kernel(
    capacity, factors_hbm, gate_ref, up_ref, down_hbm, out_ref, factors_ref, down_ref, sems
):
    loads = (
        pltpu.make_async_copy(factors_hbm, factors_ref, sems.at[0]),
        pltpu.make_async_copy(down_hbm, down_ref, sems.at[1]),
    )
    for load in loads:
        load.start()
    rows, units, width = factors_ref.shape[0], gate_ref.shape[2], out_ref.shape[1]
    loads[0].wait()
    dgate, dup, hidden = (factors_ref[:, k * units : (k + 1) * units] for k in range(3))
    grad = dot(dgate, gate_ref[0], 1, 1) + dot(dup, up_ref[0], 1, 1)
    loads[1].wait()
    back = dot(hidden, down_ref[0], 1, 0)
    groups = (rows // capacity, capacity, width)
    both = [x.astype(BF16).reshape(groups) for x in (back, grad)]
    out_ref[...] = jnp.concatenate(both, axis=1).reshape(2 * rows, width)


def combine_kernel(
    experts, capacity, ids_ref, gates_ref, grad_ref, back_ref, out_ref, dtok_ref, dgates_ref
):
    target = slots_of(ids_ref[...], experts, capacity)
    gates = column_of(gates_ref[...])
    rows = 2 * capacity * experts
    back = back_ref[...]
    slot_out = dot(hot(target, rows), back, 0, 0)
    dtok_ref[...] = dot(hot(target + capacity, rows), back, 0, 0).astype(BF16)
    out_ref[...] = (gates * slot_out).astype(BF16)
    value = jnp.sum(grad_ref[...].astype(F32) * slot_out, axis=1, keepdims=True)
    tok = value.shape[0]
    eye = iota((tok, tok), 0) == iota((tok, tok), 1)
    dgates_ref[...] = jnp.sum(jnp.where(eye, value, 0.0), axis=0, keepdims=True)


def split_kernel(in_hbm, *refs):
    outs, held, sems = refs[:3], refs[3], refs[4]
    loads = [
        pltpu.make_async_copy(in_hbm.at[k], held.at[k], sems.at[k])
        for k in range(3)
    ]
    stores = [pltpu.make_async_copy(held.at[k], outs[k].at[0], sems.at[3 + k]) for k in range(3)]
    for load in loads:
        load.start()
    for load, store in zip(loads, stores):
        load.wait()
        store.start()
    for store in stores:
        store.wait()


def call(kernel, out_shape, in_specs, out_specs, scratch, vmem_mib, flops, traffic, name):
    return pl.pallas_call(
        kernel,
        out_shape=out_shape,
        in_specs=in_specs,
        out_specs=out_specs,
        scratch_shapes=scratch,
        compiler_params=pltpu.CompilerParams(vmem_limit_bytes=vmem_mib * 2**20),
        cost_estimate=pl.CostEstimate(flops=flops, bytes_accessed=traffic, transcendentals=0),
        name=name,
    )


def in_hbm(*arrays):
    return [pltpu.with_memory_space_constraint(a, pltpu.HBM) for a in arrays]


def move_rows(buffer):
    return lax.all_to_all(buffer, ("node", "local"), split_axis=0, concat_axis=0, tiled=True)


def on_device(tokens, expert_ids, gates, out_grad, w_gate, w_up, w_down):
    experts = lax.axis_size("node") * lax.axis_size("local")
    parts = lax.axis_size("dp")
    tok, width = tokens.shape
    units = w_gate.shape[2]
    capacity = max(2, 2 * tok // experts)
    rows = experts * capacity
    sds = jax.ShapeDtypeStruct
    ids = expert_ids.reshape(1, tok)
    gate_row = gates.reshape(1, tok)
    dma = pltpu.SemaphoreType.DMA
    outgoing = call(
        functools.partial(dispatch_kernel, experts, capacity),
        sds((2 * rows, width), BF16), [HBM] * 4, VMEM,
        [pltpu.VMEM((1, tok), jnp.int32), pltpu.VMEM((1, tok), F32)]
        + [pltpu.VMEM((tok, width), BF16)] * 2 + [dma((4,))],
        12, 8 * rows * tok * width, 8 * tok * width, "dispatch",
    )(*in_hbm(ids, gate_row, tokens, out_grad))
    incoming = move_rows(outgoing.reshape(experts, 2 * capacity, width)).reshape(2 * rows, width)
    blocks = (3, units, width)
    terms, factors = call(
        functools.partial(terms_kernel, capacity),
        (pltpu.HBM(blocks, BF16), pltpu.HBM((rows, 3 * units), BF16)), [VMEM] * 4, [HBM] * 2,
        [pltpu.VMEM(blocks, BF16), pltpu.VMEM((rows, 3 * units), BF16), dma((3 * COLS + 1,))],
        20, 18 * rows * width * units, 10 * width * units + 4 * rows * width, "terms",
    )(incoming, w_gate, w_up, w_down)
    shares = lax.psum_scatter(terms, "dp", scatter_dimension=1, tiled=True)
    back = call(
        functools.partial(returns_kernel, capacity),
        sds((2 * rows, width), BF16), [HBM, VMEM, VMEM, HBM], VMEM,
        [pltpu.VMEM((rows, 3 * units), BF16), pltpu.VMEM((1, units, width), BF16), dma((2,))], 16,
        10 * rows * width * units, 6 * width * units + 4 * rows * width, "returns",
    )(*in_hbm(factors), w_gate, w_up, *in_hbm(w_down))
    back = move_rows(back.reshape(experts, 2 * capacity, width)).reshape(2 * rows, width)
    layer_out, grad_in, grad_gates = call(
        functools.partial(combine_kernel, experts, capacity),
        (sds((tok, width), BF16), sds((tok, width), BF16), sds((1, tok), F32)),
        [VMEM] * 4, [VMEM] * 3, [], 12, 8 * rows * tok * width, 10 * tok * width, "combine",
    )(ids, gate_row, out_grad, back)
    share = pltpu.HBM((1, units // parts, width), BF16)
    grads = call(
        split_kernel, (share,) * 3, [HBM], [HBM] * 3,
        [pltpu.VMEM((3, units // parts, width), BF16), dma((6,))], 4, 0, 2 * 3 * units // parts * width, "split"
    )(*in_hbm(shares))
    return (layer_out, grad_in, grad_gates.reshape(tok, 1), *grads)


def solution(mesh):
    by_token = P(("dp", "node", "local"), None)
    by_expert = P(("node", "local"), None, None)
    by_share = P(("node", "local"), "dp", None)
    return jax.shard_map(
        on_device,
        mesh=mesh,
        in_specs=(by_token,) * 4 + (by_expert,) * 3,
        out_specs=(by_token,) * 3 + (by_share,) * 3,
        check_vma=False,
    )
```
